32 devices in a mesh: fine: 16 (over z, x, core), coarse: 2 (over y).
Axes of the slice: x: 2, y: 2, z: 4, core: 2. Of those that a mesh axis runs over, the one named last changes fastest.
Arguments:
- start_states: float32 [16, 1, 16, 64, 256], P('fine', None, 'coarse'), may hold values from -6 to 6
- weights: bfloat16 [64, 9, 256, 256], P('fine'), may hold values from -0.125 to 0.125
- biases: float32 [64, 256], P('fine'), may hold values from -3 to 3
- step_sizes: float32 [64], P('fine'), may hold values from 0.1 to 0.4
Outputs:
- corrected: float32 [16, 1, 16, 64, 256], P('fine', None, 'coarse')
- slab_ends: float32 [16, 1, 16, 64, 256], P('fine', None, 'coarse')
The draws below stay inside these ranges and needn't reach their ends.
All inputs are finite; a program needn't handle non-finite values.
Results may differ from the reference program's by a relative error of at most 0.014.
Values may be sent and summed in bfloat16 or wider, within the bound.
A program may use at most 64 MiB of HBM per device.

```python
import math
import jax
import jax.numpy as jnp
from jax import lax

C = 256
LAYERS_DEV = 4
COLS = 64
BATCH = 1
SLABS = 16
LAYERS = 64
ROWS = 16
N_FINE = 16


def level_of(stream_key, shape, split, smallest, high):
    factor_of, own = 1.0, jax.random.fold_in(stream_key, 6)
    for axis_at, parts in split:
        heights = jnp.exp(jax.random.uniform(jax.random.fold_in(own, axis_at), (parts,), jnp.float32, smallest / len(split), high / len(split)))
        factor_of = factor_of * jnp.repeat(heights, shape[axis_at] // parts).reshape([-1 if axis == axis_at else 1 for axis in range(len(shape))])
    return factor_of


def scatter_about(stream_key, shape, deviation, reach, cuts=(), dtype=jnp.bfloat16):
    array = deviation * jax.random.normal(stream_key, shape, jnp.float32)
    if cuts:
        array = array * level_of(stream_key, shape, cuts, -0.22, 0.18)
    return jnp.clip(array, -reach, reach).astype(dtype)


def setup_inputs(seed: int = 0) -> dict:
    seeds = jax.random.split(jax.random.key(seed), 5)
    return {
        "start_states": scatter_about(seeds[0], (SLABS, BATCH, ROWS, COLS, C), 1.0, 6.0, ((0, 16), (2, 2)), jnp.float32),
        "weights": scatter_about(seeds[1], (LAYERS, 9, C, C), (9 * C) ** -0.5, 0.125, ((0, 16),)),
        "biases": scatter_about(seeds[2], (LAYERS, C), 0.5, 3.0, ((0, 16),), jnp.float32),
        "step_sizes": jnp.clip(jnp.exp(math.log(0.4) - 1.3862944 * jax.random.uniform(seeds[3], (LAYERS,), jnp.float32) ** level_of(seeds[3], (LAYERS,), ((0, 16),), -0.2, 0.2)), 0.1, 0.4),
    }


def conv_map(current_state, kernel):
    padded = jnp.pad(current_state.astype(jnp.bfloat16), ((0, 0), (1, 1), (1, 1), (0, 0)))
    row_count = current_state.shape[1]
    col_count = current_state.shape[2]
    channels = current_state.shape[3]
    tap_slices = [padded[:, row_shift:row_shift + row_count, col_shift:col_shift + col_count, :] for row_shift in range(3) for col_shift in range(3)]
    stacked = jnp.concatenate(tap_slices, axis=-1).reshape(-1, 9 * channels)
    product = jnp.dot(stacked, kernel.reshape(9 * channels, channels), preferred_element_type=jnp.float32)
    return product.reshape(current_state.shape)


def relax_slab(packed):
    current_state, slab_kernels, slab_biases, slab_steps = packed
    first_slope = jnp.zeros(current_state.shape, jnp.float32)
    for layer_index in range(LAYERS_DEV):
        slope_term = jnp.tanh(conv_map(current_state, slab_kernels[layer_index]) + slab_biases[layer_index])
        if layer_index == 0:
            first_slope = slope_term
        current_state = current_state + slab_steps[layer_index] * slope_term
    return current_state, first_slope


def reference(start_states, weights, biases, step_sizes):
    kernels = weights.reshape(N_FINE, LAYERS_DEV, 9, C, C)
    bias_rows = biases.reshape(N_FINE, LAYERS_DEV, C)
    step_rows = step_sizes.reshape(N_FINE, LAYERS_DEV)
    relaxed, first_slopes = lax.map(relax_slab, (start_states, kernels, bias_rows, step_rows))
    coarse_steps = jnp.sum(step_rows, axis=1)
    defects = relaxed - (start_states + coarse_steps[:, None, None, None, None] * first_slopes)

    def advance(carried, packed):
        kernel, bias_row, coarse_step, defect = packed
        following = carried + coarse_step * jnp.tanh(conv_map(carried, kernel) + bias_row) + defect
        return following, following

    ignored, chained = lax.scan(advance, start_states[0], (kernels[:-1, 0], bias_rows[:-1, 0], coarse_steps[:-1], defects[:-1]))
    corrected = jnp.concatenate([start_states[:1], chained], axis=0)
    slab_ends, unused = lax.map(relax_slab, (corrected, kernels, bias_rows, step_rows))
    return corrected, slab_ends
```

```python
import functools

import jax
import jax.numpy as jnp
from jax import lax
from jax.experimental import pallas as pl
from jax.experimental.pallas import tpu as pltpu
from jax.sharding import PartitionSpec as P

MESH = pl.DeviceIdType.MESH


def kernel(
    slabs,
    bands,
    start,
    weights,
    biases,
    steps,
    corrected,
    ends,
    cols,
    current,
    defect,
    advanced,
    inbox,
    halo,
    stage,
    row_send,
    row_recv,
    halo_send,
    halo_recv,
):
    rows, width, channels = start.shape
    layers = weights.shape[0]
    half = rows // 2
    slab = lax.axis_index("fine")
    band = lax.axis_index("coarse")
    total_step = steps[0]
    for layer in range(1, layers):
        total_step = total_step + steps[layer]

    def has_band(side):
        other = band + 2 * side - 1
        return (other >= 0) & (other < bands)

    barrier = pltpu.get_barrier_semaphore()
    around = [(i, j) for i in (-1, 0, 1) for j in (-1, 0, 1) if (i, j) != (0, 0)]
    for i, j in around:
        there = (slab + i >= 0) & (slab + i < slabs) & (band + j >= 0) & (band + j < bands)

        @pl.when(there)
        def _():
            pl.semaphore_signal(
                barrier, inc=1, device_id=(slab + i, band + j), device_id_type=MESH
            )

    def span(at, count):
        return 1 + jnp.where(at > 0, 1, 0) + jnp.where(at < count - 1, 1, 0)

    pl.semaphore_wait(barrier, span(slab, slabs) * span(band, bands) - 1)

    def widened(value):
        count = value.shape[0]
        column = lax.rem(lax.broadcasted_iota(jnp.int32, value.shape, 0), width)
        left = jnp.where(column == 0, 0.0, pltpu.roll(value, 1, 0))
        right = jnp.where(column == width - 1, 0.0, pltpu.roll(value, count - 1, 0))
        return jnp.concatenate([left, value, right], axis=-1).astype(jnp.bfloat16)

    def put(parity, place, value):
        count = value.shape[0] // width
        cols[parity, pl.ds(place, count)] = widened(value).reshape(count, width, 3 * channels)

    def slope(parity, first, count, layer):
        taps = [
            cols[parity, pl.ds(first + a, count)].reshape(count * width, 3 * channels)
            for a in range(3)
        ]
        product = jnp.dot(
            jnp.concatenate(taps, axis=-1), weights[layer], preferred_element_type=jnp.float32
        )
        return jnp.tanh(product + biases[pl.ds(layer, 1), :])

    def halo_copy(slot, side, ahead):
        return pltpu.make_async_remote_copy(
            src_ref=stage.at[slot, side],
            dst_ref=halo.at[slot, 1 - side],
            send_sem=halo_send.at[slot, side],
            recv_sem=halo_recv.at[slot, 1 - side],
            device_id=(slab + ahead, band + 2 * side - 1),
            device_id_type=MESH,
        )

    def send_halo(slot, side, value, ahead=0):
        @pl.when(has_band(side))
        def _():
            stage[slot, side] = value.astype(jnp.bfloat16)
            halo_copy(slot, side, ahead).start()

    def take_halo(slot, side, parity):
        @pl.when(has_band(side))
        def _():
            pltpu.make_async_remote_copy(
                src_ref=stage.at[slot, 1 - side],
                dst_ref=halo.at[slot, side],
                send_sem=halo_send.at[slot, 1 - side],
                recv_sem=halo_recv.at[slot, side],
                device_id=(slab, band + 2 * side - 1),
                device_id_type=MESH,
            ).wait_recv()
            put(parity, side * (rows + 1), halo[slot, side].astype(jnp.float32))

    def row_copy(row):
        return pltpu.make_async_remote_copy(
            src_ref=advanced.at[row],
            dst_ref=inbox.at[row],
            send_sem=row_send.at[row],
            recv_sem=row_recv.at[row],
            device_id=(slab + 1, band),
            device_id_type=MESH,
        )

    def layer_step(base, layer, relaxing):
        parity = lax.rem(layer, 2)

        def part(at, carry):
            side = lax.rem(at + band, 2)
            first = side * half
            take_halo(base + layer, side, parity)
            before = current[pl.ds(first, half)].reshape(half * width, channels)
            slope_term = slope(parity, first, half, layer)
            after = before + steps[layer] * slope_term
            current[pl.ds(first, half)] = after.reshape(half, width, channels)

            @pl.when(layer < layers - 1)
            def _():
                send_halo(base + layer + 1, side, current[side * (rows - 1)])
                put(1 - parity, first + 1, after)

            if relaxing:

                @pl.when(layer == 0)
                def _():
                    coarse = before + total_step * slope_term
                    defect[pl.ds(first, half)] = -coarse.reshape(half, width, channels)

                @pl.when(layer == layers - 1)
                def _():
                    defect[pl.ds(first, half)] += after.reshape(half, width, channels)

            return carry

        lax.fori_loop(0, 2, part, 0)

    for side in range(2):
        send_halo(0, side, start[side * (rows - 1)])

    @pl.when(band == 0)
    def _():
        cols[:, 0] = jnp.zeros((2, width, 3 * channels), jnp.bfloat16)

    @pl.when(band == bands - 1)
    def _():
        cols[:, rows + 1] = jnp.zeros((2, width, 3 * channels), jnp.bfloat16)

    def load(row, carry):
        current[row] = start[row]
        put(0, row + 1, start[row])
        return carry

    lax.fori_loop(0, rows, load, 0)

    def relax(layer, carry):
        layer_step(0, layer, True)
        return carry

    lax.fori_loop(0, layers, relax, 0)

    near = 1 - lax.rem(band, 2)
    far = 1 - near

    def place(at):
        return near * (rows - 1) + (1 - 2 * near) * at

    @pl.when(slab == 0)
    def _():
        def hand_on(at, carry):
            row = place(at)
            value = current[row]
            advanced[row] = value

            @pl.when(slab < slabs - 1)
            def _():
                row_copy(row).start()

                @pl.when(at == 0)
                def _():
                    send_halo(layers, near, value, 1)

                @pl.when(at == rows - 1)
                def _():
                    send_halo(layers, far, value, 1)

            return carry

        lax.fori_loop(0, rows, hand_on, 0)
        corrected[...] = start[...]
        ends[...] = current[...]

    @pl.when(slab > 0)
    def _():
        def take_row(row):
            row_copy(row).wait_recv()
            put(0, row + 1, inbox[row])

        take_row(place(0))
        take_halo(layers, near, 0)

        def chain(at, carry):
            row = place(at)

            @pl.when(at < rows - 1)
            def _():
                take_row(place(at + 1))

            @pl.when(at == rows - 1)
            def _():
                take_halo(layers, far, 0)

            slope_term = slope(0, row, 1, 0)
            value = inbox[row]
            following = value + total_step * slope_term + defect[row]

            @pl.when(slab < slabs - 1)
            def _():
                advanced[row] = following
                row_copy(row).start()

                @pl.when(at == 0)
                def _():
                    send_halo(layers, near, following, 1)

                @pl.when(at == rows - 1)
                def _():
                    send_halo(layers, far, following, 1)

            after = value + steps[0] * slope_term
            if layers > 1:

                @pl.when(at == 0)
                def _():
                    send_halo(layers + 1, near, after)

                @pl.when(at == rows - 1)
                def _():
                    send_halo(layers + 1, far, after)

            current[row] = after
            put(1, row + 1, after)
            corrected[row] = value
            return carry

        lax.fori_loop(0, rows, chain, 0)

        def finish(layer, carry):
            layer_step(layers, layer, False)
            return carry

        lax.fori_loop(1, layers, finish, 0)
        ends[...] = current[...]

    for side in range(2):

        @pl.when(has_band(side))
        def _():
            for slot in range(layers):
                halo_copy(slot, side, 0).wait_send()

            @pl.when(slab < slabs - 1)
            def _():
                halo_copy(layers, side, 1).wait_send()

            @pl.when(slab > 0)
            def _():
                for slot in range(layers + 1, 2 * layers):
                    halo_copy(slot, side, 0).wait_send()

    @pl.when(slab < slabs - 1)
    def _():
        for row in range(rows):
            row_copy(row).wait_send()


def local(start_states, weights, biases, step_sizes):
    rows, width, channels = start_states.shape[2:]
    layers = weights.shape[0]
    state = (rows, width, channels)
    slots = 2 * layers
    whole = pl.BlockSpec(memory_space=pltpu.VMEM)
    shape = jax.ShapeDtypeStruct(state, jnp.float32)
    corrected, ends = pl.pallas_call(
        functools.partial(kernel, lax.axis_size("fine"), lax.axis_size("coarse")),
        out_shape=(shape, shape),
        in_specs=[whole, whole, whole, pl.BlockSpec(memory_space=pltpu.SMEM)],
        out_specs=(whole, whole),
        scratch_shapes=[
            pltpu.VMEM((2, rows + 2, width, 3 * channels), jnp.bfloat16),
            pltpu.VMEM(state, jnp.float32),
            pltpu.VMEM(state, jnp.float32),
            pltpu.VMEM(state, jnp.float32),
            pltpu.VMEM(state, jnp.float32),
            pltpu.VMEM((slots, 2, width, channels), jnp.bfloat16),
            pltpu.VMEM((slots, 2, width, channels), jnp.bfloat16),
            pltpu.SemaphoreType.DMA((rows,)),
            pltpu.SemaphoreType.DMA((rows,)),
            pltpu.SemaphoreType.DMA((slots, 2)),
            pltpu.SemaphoreType.DMA((slots, 2)),
        ],
        compiler_params=pltpu.CompilerParams(
            collective_id=0, has_side_effects=True, vmem_limit_bytes=40 * 1024 * 1024
        ),
    )(
        start_states.reshape(state),
        weights.reshape(layers, 9 * channels, channels),
        biases,
        step_sizes,
    )
    return (corrected.reshape(start_states.shape), ends.reshape(start_states.shape))


def solution(mesh):
    in_specs = (
        P("fine", None, "coarse", None, None),
        P("fine", None, None, None),
        P("fine", None),
        P("fine"),
    )
    out_specs = (P("fine", None, "coarse", None, None), P("fine", None, "coarse", None, None))
    return jax.shard_map(local, mesh=mesh, in_specs=in_specs, out_specs=out_specs, check_vma=False)
```

```python
import functools

import jax
import jax.numpy as jnp
from jax import lax
from jax.experimental import pallas as pl
from jax.experimental.pallas import tpu as pltpu
from jax.sharding import PartitionSpec as P

MESH = pl.DeviceIdType.MESH


def kernel(
    slabs,
    bands,
    start,
    stored_weights,
    biases,
    steps,
    corrected,
    ends,
    cols,
    current,
    defect,
    advanced,
    inbox,
    halo,
    stage,
    row_send,
    row_recv,
    halo_send,
    halo_recv,
    weights,
    load_sem,
):
    rows, width, channels = start.shape
    layers = weights.shape[0]
    window = min(2, rows)
    state_load = pltpu.make_async_copy(start, current, load_sem.at[layers])
    state_load.start()

    def weight_load(layer):
        return pltpu.make_async_copy(
            stored_weights.at[layer], weights.at[layer], load_sem.at[layer]
        )

    for layer in range(layers):
        weight_load(layer).start()

    half = rows // 2
    slab = lax.axis_index("fine")
    band = lax.axis_index("coarse")
    total_step = steps[0]
    for layer in range(1, layers):
        total_step = total_step + steps[layer]

    def has_band(side):
        other = band + 2 * side - 1
        return (other >= 0) & (other < bands)

    barrier = pltpu.get_barrier_semaphore()
    around = [(i, j) for i in (-1, 0, 1) for j in (-1, 0, 1) if (i, j) != (0, 0)]
    for i, j in around:
        there = (slab + i >= 0) & (slab + i < slabs) & (band + j >= 0) & (band + j < bands)

        @pl.when(there)
        def _():
            pl.semaphore_signal(
                barrier, inc=1, device_id=(slab + i, band + j), device_id_type=MESH
            )

    def span(at, count):
        return 1 + jnp.where(at > 0, 1, 0) + jnp.where(at < count - 1, 1, 0)

    pl.semaphore_wait(barrier, span(slab, slabs) * span(band, bands) - 1)

    def widened(value):
        count = value.shape[0]
        column = lax.rem(lax.broadcasted_iota(jnp.int32, value.shape, 0), width)
        left = jnp.where(column == 0, 0.0, pltpu.roll(value, 1, 0))
        right = jnp.where(column == width - 1, 0.0, pltpu.roll(value, count - 1, 0))
        return jnp.concatenate([left, value, right], axis=-1).astype(jnp.bfloat16)

    def put(parity, place, value):
        count = value.shape[0] // width
        cols[parity, pl.ds(place, count)] = widened(value).reshape(count, width, 3 * channels)

    def slope(parity, first, count, layer):
        taps = [
            cols[parity, pl.ds(first + a, count)].reshape(count * width, 3 * channels)
            for a in range(3)
        ]
        product = jnp.dot(
            jnp.concatenate(taps, axis=-1), weights[layer], preferred_element_type=jnp.float32
        )
        return jnp.tanh(product + biases[pl.ds(layer, 1), :])

    def halo_copy(slot, side, ahead):
        return pltpu.make_async_remote_copy(
            src_ref=stage.at[slot, side],
            dst_ref=halo.at[slot, 1 - side],
            send_sem=halo_send.at[slot, side],
            recv_sem=halo_recv.at[slot, 1 - side],
            device_id=(slab + ahead, band + 2 * side - 1),
            device_id_type=MESH,
        )

    def send_halo(slot, side, value, ahead=0):
        @pl.when(has_band(side))
        def _():
            stage[slot, side] = value.astype(jnp.bfloat16)
            halo_copy(slot, side, ahead).start()

    def take_halo(slot, side, parity):
        @pl.when(has_band(side))
        def _():
            pltpu.make_async_remote_copy(
                src_ref=stage.at[slot, 1 - side],
                dst_ref=halo.at[slot, side],
                send_sem=halo_send.at[slot, 1 - side],
                recv_sem=halo_recv.at[slot, side],
                device_id=(slab, band + 2 * side - 1),
                device_id_type=MESH,
            ).wait_recv()
            put(parity, side * (rows + 1), halo[slot, side].astype(jnp.float32))

    def row_copy(row):
        return pltpu.make_async_remote_copy(
            src_ref=advanced.at[row],
            dst_ref=inbox.at[row],
            send_sem=row_send.at[row],
            recv_sem=row_recv.at[row],
            device_id=(slab + 1, band),
            device_id_type=MESH,
        )

    def layer_step(base, layer, relaxing):
        parity = lax.rem(layer, 2)

        def part(at, carry):
            side = lax.rem(at + band, 2)
            first = side * half
            take_halo(base + layer, side, parity)
            before = current[pl.ds(first, half)].reshape(half * width, channels)
            slope_term = slope(parity, first, half, layer)
            after = before + steps[layer] * slope_term
            current[pl.ds(first, half)] = after.reshape(half, width, channels)

            @pl.when(layer < layers - 1)
            def _():
                send_halo(base + layer + 1, side, current[side * (rows - 1)])
                put(1 - parity, first + 1, after)

            if relaxing:

                @pl.when(layer == 0)
                def _():
                    coarse = before + total_step * slope_term
                    defect[pl.ds(first, half)] = -coarse.reshape(half, width, channels)

                @pl.when(layer == layers - 1)
                def _():
                    defect[pl.ds(first, half)] += after.reshape(half, width, channels)

            return carry

        lax.fori_loop(0, 2, part, 0)

    first_load = pltpu.make_async_copy(start, corrected, load_sem.at[layers + 1])

    @pl.when(slab == 0)
    def _():
        first_load.start()

    state_load.wait()
    for side in range(2):
        send_halo(0, side, current[side * (rows - 1)])

    @pl.when(band == 0)
    def _():
        cols[:, 0] = jnp.zeros((2, width, 3 * channels), jnp.bfloat16)

    @pl.when(band == bands - 1)
    def _():
        cols[:, rows + 1] = jnp.zeros((2, width, 3 * channels), jnp.bfloat16)

    def load(row, carry):
        put(0, row + 1, current[row])
        return carry

    lax.fori_loop(0, rows, load, 0)

    def relax(layer, carry):
        weight_load(layer).wait()
        layer_step(0, layer, True)
        return carry

    lax.fori_loop(0, layers, relax, 0)

    near = 1 - lax.rem(band, 2)
    far = 1 - near

    def place(at):
        return near * (rows - 1) + (1 - 2 * near) * at

    def send_row(at):
        @pl.when(at >= window)
        def _():
            row_copy(place(at - window)).wait_send()

        row_copy(place(at)).start()

    @pl.when(slab == 0)
    def _():
        def hand_on(at, carry):
            row = place(at)
            value = current[row]
            advanced[row] = value

            @pl.when(slab < slabs - 1)
            def _():
                send_row(at)

                @pl.when(at == 0)
                def _():
                    send_halo(layers, near, value, 1)

                @pl.when(at == rows - 1)
                def _():
                    send_halo(layers, far, value, 1)

            return carry

        lax.fori_loop(0, rows, hand_on, 0)
        first_load.wait()
        ends[...] = current[...]

    @pl.when(slab > 0)
    def _():
        def take_row(row):
            row_copy(row).wait_recv()
            put(0, row + 1, inbox[row])

        take_row(place(0))
        take_halo(layers, near, 0)

        def chain(at, carry):
            row = place(at)

            @pl.when(at < rows - 1)
            def _():
                take_row(place(at + 1))

            @pl.when(at == rows - 1)
            def _():
                take_halo(layers, far, 0)

            slope_term = slope(0, row, 1, 0)
            value = inbox[row]
            following = value + total_step * slope_term + defect[row]

            @pl.when(slab < slabs - 1)
            def _():
                advanced[row] = following
                send_row(at)

                @pl.when(at == 0)
                def _():
                    send_halo(layers, near, following, 1)

                @pl.when(at == rows - 1)
                def _():
                    send_halo(layers, far, following, 1)

            after = value + steps[0] * slope_term
            if layers > 1:

                @pl.when(at == 0)
                def _():
                    send_halo(layers + 1, near, after)

                @pl.when(at == rows - 1)
                def _():
                    send_halo(layers + 1, far, after)

            current[row] = after
            put(1, row + 1, after)
            corrected[row] = value
            return carry

        lax.fori_loop(0, rows, chain, 0)

        def finish(layer, carry):
            layer_step(layers, layer, False)
            return carry

        lax.fori_loop(1, layers, finish, 0)
        ends[...] = current[...]

    for side in range(2):

        @pl.when(has_band(side))
        def _():
            for slot in range(layers):
                halo_copy(slot, side, 0).wait_send()

            @pl.when(slab < slabs - 1)
            def _():
                halo_copy(layers, side, 1).wait_send()

            @pl.when(slab > 0)
            def _():
                for slot in range(layers + 1, 2 * layers):
                    halo_copy(slot, side, 0).wait_send()

    @pl.when(slab < slabs - 1)
    def _():
        for at in range(rows - window, rows):
            row_copy(place(at)).wait_send()


def local(start_states, weights, biases, step_sizes):
    rows, width, channels = start_states.shape[2:]
    layers = weights.shape[0]
    state = (rows, width, channels)
    slots = 2 * layers
    anywhere = pl.BlockSpec(memory_space=pl.ANY)
    whole = pl.BlockSpec(memory_space=pltpu.VMEM)
    shape = jax.ShapeDtypeStruct(state, jnp.float32)
    corrected, ends = pl.pallas_call(
        functools.partial(kernel, lax.axis_size("fine"), lax.axis_size("coarse")),
        out_shape=(shape, shape),
        in_specs=[anywhere, anywhere, whole, pl.BlockSpec(memory_space=pltpu.SMEM)],
        out_specs=(whole, whole),
        scratch_shapes=[
            pltpu.VMEM((2, rows + 2, width, 3 * channels), jnp.bfloat16),
            pltpu.VMEM(state, jnp.float32),
            pltpu.VMEM(state, jnp.float32),
            pltpu.VMEM(state, jnp.float32),
            pltpu.VMEM(state, jnp.float32),
            pltpu.VMEM((slots, 2, width, channels), jnp.bfloat16),
            pltpu.VMEM((slots, 2, width, channels), jnp.bfloat16),
            pltpu.SemaphoreType.DMA((rows,)),
            pltpu.SemaphoreType.DMA((rows,)),
            pltpu.SemaphoreType.DMA((slots, 2)),
            pltpu.SemaphoreType.DMA((slots, 2)),
            pltpu.VMEM((layers, 9 * channels, channels), jnp.bfloat16),
            pltpu.SemaphoreType.DMA((layers + 2,)),
        ],
        compiler_params=pltpu.CompilerParams(
            collective_id=0, has_side_effects=True, vmem_limit_bytes=56 * 1024 * 1024
        ),
    )(
        start_states.reshape(state),
        weights.reshape(layers, 9 * channels, channels),
        biases,
        step_sizes,
    )
    return (corrected.reshape(start_states.shape), ends.reshape(start_states.shape))


def solution(mesh):
    in_specs = (
        P("fine", None, "coarse", None, None),
        P("fine", None, None, None),
        P("fine", None),
        P("fine"),
    )
    out_specs = (P("fine", None, "coarse", None, None), P("fine", None, "coarse", None, None))
    return jax.shard_map(local, mesh=mesh, in_specs=in_specs, out_specs=out_specs, check_vma=False)
```

```python
import functools

import jax
import jax.numpy as jnp
from jax import lax
from jax.experimental import pallas as pl
from jax.experimental.pallas import tpu as pltpu
from jax.sharding import PartitionSpec as P

MESH = pl.DeviceIdType.MESH


def kernel(
    slabs,
    bands,
    start,
    stored_weights,
    biases,
    steps,
    corrected,
    ends,
    cols,
    current,
    defect,
    advanced,
    inbox,
    narrow,
    narrow_inbox,
    edge,
    halo,
    row_send,
    row_recv,
    halo_send,
    halo_recv,
    weights,
    load_sem,
):
    rows, width, channels = start.shape
    layers = weights.shape[0]
    own = pl.ds(layers, rows)
    state_load = pltpu.make_async_copy(start, current.at[own], load_sem.at[layers])
    state_load.start()

    def weight_load(layer):
        return pltpu.make_async_copy(
            stored_weights.at[layer], weights.at[layer], load_sem.at[layer]
        )

    for layer in range(layers):
        weight_load(layer).start()

    slab = lax.axis_index("fine")
    band = lax.axis_index("coarse")
    total_step = steps[0]
    for layer in range(1, layers):
        total_step = total_step + steps[layer]

    def has_band(side):
        other = band + 2 * side - 1
        return (other >= 0) & (other < bands)

    barrier = pltpu.get_barrier_semaphore()
    around = [(i, j) for i in (-1, 0, 1) for j in (-1, 0, 1) if (i, j) != (0, 0)]
    for i, j in around:
        there = (slab + i >= 0) & (slab + i < slabs) & (band + j >= 0) & (band + j < bands)

        @pl.when(there)
        def _():
            pl.semaphore_signal(
                barrier, inc=1, device_id=(slab + i, band + j), device_id_type=MESH
            )

    def span(at, count):
        return 1 + jnp.where(at > 0, 1, 0) + jnp.where(at < count - 1, 1, 0)

    pl.semaphore_wait(barrier, span(slab, slabs) * span(band, bands) - 1)

    def widened(value):
        count = value.shape[0]
        column = lax.rem(lax.broadcasted_iota(jnp.int32, value.shape, 0), width)
        left = jnp.where(column == 0, 0.0, pltpu.roll(value, 1, 0))
        right = jnp.where(column == width - 1, 0.0, pltpu.roll(value, count - 1, 0))
        return jnp.concatenate([left, value, right], axis=-1).astype(jnp.bfloat16)

    def put(parity, place, value):
        count = value.shape[0] // width
        cols[parity, pl.ds(place, count)] = widened(value).reshape(count, width, 3 * channels)

    def slope(parity, first, count, layer):
        taps = [
            cols[parity, pl.ds(first + a, count)].reshape(count * width, 3 * channels)
            for a in range(3)
        ]
        product = jnp.dot(
            jnp.concatenate(taps, axis=-1), weights[layer], preferred_element_type=jnp.float32
        )
        return jnp.tanh(product + biases[pl.ds(layer, 1), :])

    first_load = pltpu.make_async_copy(start, corrected, load_sem.at[layers + 1])

    @pl.when(slab == 0)
    def _():
        first_load.start()

    def margin_copy(side):
        return pltpu.make_async_remote_copy(
            src_ref=edge.at[side],
            dst_ref=halo.at[0, 1 - side],
            send_sem=halo_send.at[0, side, 0],
            recv_sem=halo_recv.at[0, 1 - side, 0],
            device_id=(slab, band + 2 * side - 1),
            device_id_type=MESH,
        )

    def cross_copy(side, at):
        return pltpu.make_async_remote_copy(
            src_ref=narrow.at[side * (rows - layers) + at],
            dst_ref=halo.at[1, 1 - side, at],
            send_sem=halo_send.at[1, side, at],
            recv_sem=halo_recv.at[1, 1 - side, at],
            device_id=(slab + 1, band + 2 * side - 1),
            device_id_type=MESH,
        )

    def wide_copy(row):
        return pltpu.make_async_remote_copy(
            src_ref=advanced.at[row],
            dst_ref=inbox.at[row],
            send_sem=row_send.at[row],
            recv_sem=row_recv.at[row],
            device_id=(slab + 1, band),
            device_id_type=MESH,
        )

    def narrow_copy(row):
        return pltpu.make_async_remote_copy(
            src_ref=narrow.at[row],
            dst_ref=narrow_inbox.at[row],
            send_sem=row_send.at[row],
            recv_sem=row_recv.at[row],
            device_id=(slab + 1, band),
            device_id_type=MESH,
        )

    odd = lax.rem(slab, 2)

    def send_row(row, value):
        narrow[row] = value.astype(jnp.bfloat16)

        @pl.when(odd == 1)
        def _():
            narrow_copy(row).start()

        @pl.when(odd == 0)
        def _():
            advanced[row] = value
            wide_copy(row).start()

        for side in range(2):
            at = row - side * (rows - layers)

            @pl.when(has_band(side) & (at >= 0) & (at < layers))
            def _():
                cross_copy(side, at).start()

    def set_margin(phase, side, at):
        value = halo[phase, side, at].astype(jnp.float32)
        spot = side * (layers + rows) + at
        current[spot] = value
        put(0, spot, value)

    def take_cross(side, at):
        @pl.when(has_band(side))
        def _():
            pltpu.make_async_remote_copy(
                src_ref=narrow.at[at],
                dst_ref=halo.at[1, side, at],
                send_sem=halo_send.at[1, 1 - side, at],
                recv_sem=halo_recv.at[1, side, at],
                device_id=(slab, band + 2 * side - 1),
                device_id_type=MESH,
            ).wait_recv()
            set_margin(1, side, at)

    def layer_step(layer, relaxing):
        margin = layers - 1 - layer
        parity = layer % 2
        if bands == 1:
            first, count = layers, rows
        elif bands == 2:
            first, count = layers - margin * band, rows + margin
        else:
            first, count = layers - margin, rows + 2 * margin
        before = current[pl.ds(first, count)].reshape(count * width, channels)
        slope_term = slope(parity, first - 1, count, layer)
        after = before + steps[layer] * slope_term
        if bands > 2:
            spot = first + lax.broadcasted_iota(jnp.int32, after.shape, 0) // width
            outside = ((band == 0) & (spot < layers)) | (
                (band == bands - 1) & (spot >= layers + rows)
            )
            after = jnp.where(outside, 0.0, after)
        current[pl.ds(first, count)] = after.reshape(count, width, channels)
        if layer < layers - 1:
            put(1 - parity, first, after)
        if relaxing and layer == 0:
            coarse = (before + total_step * slope_term).reshape(count, width, channels)
            if bands == 2:

                @pl.when(band == 0)
                def _():
                    defect[...] = -coarse[:rows]

                @pl.when(band == 1)
                def _():
                    defect[...] = -coarse[margin:]
            else:
                defect[...] = -coarse[layers - first : layers - first + rows]

    for side in range(2):

        @pl.when(~has_band(side))
        def _():
            spots = pl.ds(side * (layers + rows), layers)
            cols[:, spots] = jnp.zeros((2, layers, width, 3 * channels), jnp.bfloat16)
            current[spots] = jnp.zeros((layers, width, channels), jnp.float32)

    state_load.wait()
    for side in range(2):

        @pl.when(has_band(side))
        def _():
            spots = pl.ds(layers + side * (rows - layers), layers)
            edge[side] = current[spots].astype(jnp.bfloat16)
            margin_copy(side).start()

    def load(row, carry):
        put(0, layers + row, current[layers + row])
        return carry

    lax.fori_loop(0, rows, load, 0)
    for side in range(2):

        @pl.when(has_band(side))
        def _():
            pltpu.make_async_remote_copy(
                src_ref=edge.at[1 - side],
                dst_ref=halo.at[0, side],
                send_sem=halo_send.at[0, 1 - side, 0],
                recv_sem=halo_recv.at[0, side, 0],
                device_id=(slab, band + 2 * side - 1),
                device_id_type=MESH,
            ).wait_recv()
            for at in range(layers):
                set_margin(0, side, at)

    for layer in range(layers):
        weight_load(layer).wait()
        layer_step(layer, True)
    defect[...] += current[own]

    near = 1 - lax.rem(band, 2)
    far = 1 - near

    def place(at):
        return near * (rows - 1) + (1 - 2 * near) * at

    def next_to(side):
        return (1 - side) * (layers - 1)

    @pl.when(slab == 0)
    def _():
        if slabs > 1:

            def hand_on(at, carry):
                row = place(at)
                send_row(row, current[layers + row])
                return carry

            lax.fori_loop(0, rows, hand_on, 0)
        first_load.wait()
        ends[...] = current[own]

    @pl.when(slab > 0)
    def _():
        def take_row(row):
            @pl.when(odd == 1)
            def _():
                wide_copy(row).wait_recv()

            @pl.when(odd == 0)
            def _():
                narrow_copy(row).wait_recv()
                inbox[row] = narrow_inbox[row].astype(jnp.float32)

            put(0, layers + row, inbox[row])

        take_row(place(0))
        take_cross(near, next_to(near))

        def chain(at, carry):
            row = place(at)

            @pl.when(at < rows - 1)
            def _():
                take_row(place(at + 1))

            @pl.when(at == rows - 1)
            def _():
                take_cross(far, next_to(far))

            slope_term = slope(0, layers + row - 1, 1, 0)
            value = inbox[row]

            @pl.when(slab < slabs - 1)
            def _():
                send_row(row, value + total_step * slope_term + defect[row])

            after = value + steps[0] * slope_term
            current[layers + row] = after
            put(1, layers + row, after)
            corrected[row] = value
            return carry

        lax.fori_loop(0, rows, chain, 0)
        if layers > 1:
            for side in range(2):
                for at in range(layers):
                    if at != next_to(side):
                        take_cross(side, at)

                @pl.when(has_band(side))
                def _():
                    first = 1 + side * (layers + rows - 1)
                    count = layers - 1
                    before = current[pl.ds(first, count)].reshape(count * width, channels)
                    after = before + steps[0] * slope(0, first - 1, count, 0)
                    current[pl.ds(first, count)] = after.reshape(count, width, channels)
                    put(1, first, after)

            for layer in range(1, layers):
                layer_step(layer, False)
        ends[...] = current[own]

    for side in range(2):

        @pl.when(has_band(side))
        def _():
            margin_copy(side).wait_send()

            @pl.when(slab < slabs - 1)
            def _():
                for at in range(layers):
                    cross_copy(side, at).wait_send()

    @pl.when((slab < slabs - 1) & (odd == 1))
    def _():
        for row in range(rows):
            narrow_copy(row).wait_send()

    @pl.when((slab < slabs - 1) & (odd == 0))
    def _():
        for row in range(rows):
            wide_copy(row).wait_send()


def local(start_states, weights, biases, step_sizes):
    rows, width, channels = start_states.shape[2:]
    layers = weights.shape[0]
    state = (rows, width, channels)
    anywhere = pl.BlockSpec(memory_space=pl.ANY)
    whole = pl.BlockSpec(memory_space=pltpu.VMEM)
    shape = jax.ShapeDtypeStruct(state, jnp.float32)
    corrected, ends = pl.pallas_call(
        functools.partial(kernel, lax.axis_size("fine"), lax.axis_size("coarse")),
        out_shape=(shape, shape),
        in_specs=[anywhere, anywhere, whole, pl.BlockSpec(memory_space=pltpu.SMEM)],
        out_specs=(whole, whole),
        scratch_shapes=[
            pltpu.VMEM((2, rows + 2 * layers, width, 3 * channels), jnp.bfloat16),
            pltpu.VMEM((rows + 2 * layers, width, channels), jnp.float32),
            pltpu.VMEM(state, jnp.float32),
            pltpu.VMEM(state, jnp.float32),
            pltpu.VMEM(state, jnp.float32),
            pltpu.VMEM(state, jnp.bfloat16),
            pltpu.VMEM(state, jnp.bfloat16),
            pltpu.VMEM((2, layers, width, channels), jnp.bfloat16),
            pltpu.VMEM((2, 2, layers, width, channels), jnp.bfloat16),
            pltpu.SemaphoreType.DMA((rows,)),
            pltpu.SemaphoreType.DMA((rows,)),
            pltpu.SemaphoreType.DMA((2, 2, layers)),
            pltpu.SemaphoreType.DMA((2, 2, layers)),
            pltpu.VMEM((layers, 9 * channels, channels), jnp.bfloat16),
            pltpu.SemaphoreType.DMA((layers + 2,)),
        ],
        compiler_params=pltpu.CompilerParams(
            collective_id=0, has_side_effects=True, vmem_limit_bytes=56 * 1024 * 1024
        ),
    )(
        start_states.reshape(state),
        weights.reshape(layers, 9 * channels, channels),
        biases,
        step_sizes,
    )
    return (corrected.reshape(start_states.shape), ends.reshape(start_states.shape))


def solution(mesh):
    in_specs = (
        P("fine", None, "coarse", None, None),
        P("fine", None, None, None),
        P("fine", None),
        P("fine"),
    )
    out_specs = (P("fine", None, "coarse", None, None), P("fine", None, "coarse", None, None))
    return jax.shard_map(local, mesh=mesh, in_specs=in_specs, out_specs=out_specs, check_vma=False)
```

```python
import functools

import jax
import jax.numpy as jnp
from jax import lax
from jax.experimental import pallas as pl
from jax.experimental.pallas import tpu as pltpu
from jax.sharding import PartitionSpec as P

MESH = pl.DeviceIdType.MESH


def kernel(
    slabs,
    bands,
    start,
    stored_weights,
    biases,
    steps,
    corrected,
    ends,
    cols,
    current,
    defect,
    advanced,
    inbox,
    narrow,
    narrow_inbox,
    edge,
    halo,
    row_send,
    row_recv,
    halo_send,
    halo_recv,
    weights,
    load_sem,
):
    rows, width, channels = start.shape
    layers = weights.shape[0]
    own = pl.ds(layers, rows)
    state_load = pltpu.make_async_copy(start, current.at[own], load_sem.at[layers])
    state_load.start()

    def weight_load(layer):
        return pltpu.make_async_copy(
            stored_weights.at[layer], weights.at[layer], load_sem.at[layer]
        )

    weight_load(0).start()

    slab = lax.axis_index("fine")
    band = lax.axis_index("coarse")
    total_step = steps[0]
    for layer in range(1, layers):
        total_step = total_step + steps[layer]

    def has_band(side):
        other = band + 2 * side - 1
        return (other >= 0) & (other < bands)

    barrier = pltpu.get_barrier_semaphore()
    around = [(i, j) for i in (-1, 0, 1) for j in (-1, 0, 1) if (i, j) != (0, 0)]
    for i, j in around:
        there = (slab + i >= 0) & (slab + i < slabs) & (band + j >= 0) & (band + j < bands)

        @pl.when(there)
        def _():
            pl.semaphore_signal(
                barrier, inc=1, device_id=(slab + i, band + j), device_id_type=MESH
            )

    def span(at, count):
        return 1 + jnp.where(at > 0, 1, 0) + jnp.where(at < count - 1, 1, 0)

    pl.semaphore_wait(barrier, span(slab, slabs) * span(band, bands) - 1)

    def widened(value):
        count = value.shape[0]
        column = lax.rem(lax.broadcasted_iota(jnp.int32, value.shape, 0), width)
        left = jnp.where(column == 0, 0.0, pltpu.roll(value, 1, 0))
        right = jnp.where(column == width - 1, 0.0, pltpu.roll(value, count - 1, 0))
        return jnp.concatenate([left, value, right], axis=-1).astype(jnp.bfloat16)

    def put(parity, place, value):
        count = value.shape[0] // width
        cols[parity, pl.ds(place, count)] = widened(value).reshape(count, width, 3 * channels)

    def slope(parity, first, count, layer):
        taps = [
            cols[parity, pl.ds(first + a, count)].reshape(count * width, 3 * channels)
            for a in range(3)
        ]
        product = jnp.dot(
            jnp.concatenate(taps, axis=-1), weights[layer], preferred_element_type=jnp.float32
        )
        return jnp.tanh(product + biases[pl.ds(layer, 1), :])

    first_load = pltpu.make_async_copy(start, corrected, load_sem.at[layers + 1])

    @pl.when(slab == 0)
    def _():
        first_load.start()

    def margin_copy(side):
        return pltpu.make_async_remote_copy(
            src_ref=edge.at[side],
            dst_ref=halo.at[0, 1 - side],
            send_sem=halo_send.at[0, side, 0],
            recv_sem=halo_recv.at[0, 1 - side, 0],
            device_id=(slab, band + 2 * side - 1),
            device_id_type=MESH,
        )

    def cross_copy(side, at):
        return pltpu.make_async_remote_copy(
            src_ref=narrow.at[side * (rows - layers) + at],
            dst_ref=halo.at[1, 1 - side, at],
            send_sem=halo_send.at[1, side, at],
            recv_sem=halo_recv.at[1, 1 - side, at],
            device_id=(slab + 1, band + 2 * side - 1),
            device_id_type=MESH,
        )

    def wide_copy(row):
        return pltpu.make_async_remote_copy(
            src_ref=advanced.at[row],
            dst_ref=inbox.at[row],
            send_sem=row_send.at[row],
            recv_sem=row_recv.at[row],
            device_id=(slab + 1, band),
            device_id_type=MESH,
        )

    def narrow_copy(row):
        return pltpu.make_async_remote_copy(
            src_ref=narrow.at[row],
            dst_ref=narrow_inbox.at[row],
            send_sem=row_send.at[row],
            recv_sem=row_recv.at[row],
            device_id=(slab + 1, band),
            device_id_type=MESH,
        )

    odd = lax.rem(slab, 2)

    def send_row(row, value):
        narrow[row] = value.astype(jnp.bfloat16)

        @pl.when(odd == 1)
        def _():
            narrow_copy(row).start()

        @pl.when(odd == 0)
        def _():
            advanced[row] = value
            wide_copy(row).start()

        for side in range(2):
            at = row - side * (rows - layers)

            @pl.when(has_band(side) & (at >= 0) & (at < layers))
            def _():
                cross_copy(side, at).start()

    def set_margin(phase, side, at):
        value = halo[phase, side, at].astype(jnp.float32)
        spot = side * (layers + rows) + at
        current[spot] = value
        put(0, spot, value)

    def take_cross(side, at):
        @pl.when(has_band(side))
        def _():
            pltpu.make_async_remote_copy(
                src_ref=narrow.at[at],
                dst_ref=halo.at[1, side, at],
                send_sem=halo_send.at[1, 1 - side, at],
                recv_sem=halo_recv.at[1, side, at],
                device_id=(slab, band + 2 * side - 1),
                device_id_type=MESH,
            ).wait_recv()
            set_margin(1, side, at)

    def layer_step(layer, relaxing):
        margin = layers - 1 - layer
        parity = layer % 2
        if bands == 1:
            first, count = layers, rows
        elif bands == 2:
            first, count = layers - margin * band, rows + margin
        else:
            first, count = layers - margin, rows + 2 * margin
        before = current[pl.ds(first, count)].reshape(count * width, channels)
        slope_term = slope(parity, first - 1, count, layer)
        after = before + steps[layer] * slope_term
        if bands > 2:
            spot = first + lax.broadcasted_iota(jnp.int32, after.shape, 0) // width
            outside = ((band == 0) & (spot < layers)) | (
                (band == bands - 1) & (spot >= layers + rows)
            )
            after = jnp.where(outside, 0.0, after)
        current[pl.ds(first, count)] = after.reshape(count, width, channels)
        if layer < layers - 1:
            put(1 - parity, first, after)
        if relaxing and layer == 0:
            coarse = (before + total_step * slope_term).reshape(count, width, channels)
            if bands == 2:

                @pl.when(band == 0)
                def _():
                    defect[...] = -coarse[:rows]

                @pl.when(band == 1)
                def _():
                    defect[...] = -coarse[margin:]
            else:
                defect[...] = -coarse[layers - first : layers - first + rows]

    for side in range(2):

        @pl.when(~has_band(side))
        def _():
            spots = pl.ds(side * (layers + rows), layers)
            cols[:, spots] = jnp.zeros((2, layers, width, 3 * channels), jnp.bfloat16)
            current[spots] = jnp.zeros((layers, width, channels), jnp.float32)

    state_load.wait()
    for side in range(2):

        @pl.when(has_band(side))
        def _():
            spots = pl.ds(layers + side * (rows - layers), layers)
            edge[side] = current[spots].astype(jnp.bfloat16)
            margin_copy(side).start()

    def load(row, carry):
        put(0, layers + row, current[layers + row])
        return carry

    lax.fori_loop(0, rows, load, 0)
    for side in range(2):

        @pl.when(has_band(side))
        def _():
            pltpu.make_async_remote_copy(
                src_ref=edge.at[1 - side],
                dst_ref=halo.at[0, side],
                send_sem=halo_send.at[0, 1 - side, 0],
                recv_sem=halo_recv.at[0, side, 0],
                device_id=(slab, band + 2 * side - 1),
                device_id_type=MESH,
            ).wait_recv()
            for at in range(layers):
                set_margin(0, side, at)

    for layer in range(layers):
        weight_load(layer).wait()
        if layer < layers - 1:
            weight_load(layer + 1).start()
        layer_step(layer, True)
    defect[...] += current[own]

    near = 1 - lax.rem(band, 2)
    far = 1 - near

    def place(at):
        return near * (rows - 1) + (1 - 2 * near) * at

    def next_to(side):
        return (1 - side) * (layers - 1)

    @pl.when(slab == 0)
    def _():
        if slabs > 1:

            def hand_on(at, carry):
                row = place(at)
                send_row(row, current[layers + row])
                return carry

            lax.fori_loop(0, rows, hand_on, 0)
        first_load.wait()
        ends[...] = current[own]

    @pl.when(slab > 0)
    def _():
        def take_row(row):
            @pl.when(odd == 1)
            def _():
                wide_copy(row).wait_recv()

            @pl.when(odd == 0)
            def _():
                narrow_copy(row).wait_recv()
                inbox[row] = narrow_inbox[row].astype(jnp.float32)

            put(0, layers + row, inbox[row])

        def taps(row, first, count):
            read = [cols[0, layers + row - 1 + first + a] for a in range(count)]
            begin = pl.multiple_of(first * 3 * channels, 3 * channels)
            return jnp.dot(
                jnp.concatenate(read, axis=-1) if count > 1 else read[0],
                weights[0, pl.ds(begin, count * 3 * channels)],
                preferred_element_type=jnp.float32,
            )

        take_row(place(0))
        take_cross(near, next_to(near))

        def chain(at, carry):
            row = place(at)
            early = taps(row, near, 2)

            @pl.when(at < rows - 1)
            def _():
                take_row(place(at + 1))

            @pl.when(at == rows - 1)
            def _():
                take_cross(far, next_to(far))

            slope_term = jnp.tanh(early + taps(row, 2 * far, 1) + biases[0:1, :])
            value = inbox[row]

            @pl.when(slab < slabs - 1)
            def _():
                send_row(row, value + total_step * slope_term + defect[row])

            after = value + steps[0] * slope_term
            current[layers + row] = after
            put(1, layers + row, after)
            corrected[row] = value
            return carry

        lax.fori_loop(0, rows, chain, 0)
        if layers > 1:
            for side in range(2):
                for at in range(layers):
                    if at != next_to(side):
                        take_cross(side, at)

                @pl.when(has_band(side))
                def _():
                    first = 1 + side * (layers + rows - 1)
                    count = layers - 1
                    before = current[pl.ds(first, count)].reshape(count * width, channels)
                    after = before + steps[0] * slope(0, first - 1, count, 0)
                    current[pl.ds(first, count)] = after.reshape(count, width, channels)
                    put(1, first, after)

            for layer in range(1, layers):
                layer_step(layer, False)
        ends[...] = current[own]

    for side in range(2):

        @pl.when(has_band(side))
        def _():
            margin_copy(side).wait_send()

            @pl.when(slab < slabs - 1)
            def _():
                for at in range(layers):
                    cross_copy(side, at).wait_send()

    @pl.when((slab < slabs - 1) & (odd == 1))
    def _():
        for row in range(rows):
            narrow_copy(row).wait_send()

    @pl.when((slab < slabs - 1) & (odd == 0))
    def _():
        for row in range(rows):
            wide_copy(row).wait_send()


def local(start_states, weights, biases, step_sizes):
    rows, width, channels = start_states.shape[2:]
    layers = weights.shape[0]
    state = (rows, width, channels)
    anywhere = pl.BlockSpec(memory_space=pl.ANY)
    whole = pl.BlockSpec(memory_space=pltpu.VMEM)
    shape = jax.ShapeDtypeStruct(state, jnp.float32)
    corrected, ends = pl.pallas_call(
        functools.partial(kernel, lax.axis_size("fine"), lax.axis_size("coarse")),
        out_shape=(shape, shape),
        in_specs=[anywhere, anywhere, whole, pl.BlockSpec(memory_space=pltpu.SMEM)],
        out_specs=(whole, whole),
        scratch_shapes=[
            pltpu.VMEM((2, rows + 2 * layers, width, 3 * channels), jnp.bfloat16),
            pltpu.VMEM((rows + 2 * layers, width, channels), jnp.float32),
            pltpu.VMEM(state, jnp.float32),
            pltpu.VMEM(state, jnp.float32),
            pltpu.VMEM(state, jnp.float32),
            pltpu.VMEM(state, jnp.bfloat16),
            pltpu.VMEM(state, jnp.bfloat16),
            pltpu.VMEM((2, layers, width, channels), jnp.bfloat16),
            pltpu.VMEM((2, 2, layers, width, channels), jnp.bfloat16),
            pltpu.SemaphoreType.DMA((rows,)),
            pltpu.SemaphoreType.DMA((rows,)),
            pltpu.SemaphoreType.DMA((2, 2, layers)),
            pltpu.SemaphoreType.DMA((2, 2, layers)),
            pltpu.VMEM((layers, 9 * channels, channels), jnp.bfloat16),
            pltpu.SemaphoreType.DMA((layers + 2,)),
        ],
        compiler_params=pltpu.CompilerParams(
            collective_id=0, has_side_effects=True, vmem_limit_bytes=52 * 1024 * 1024
        ),
    )(
        start_states.reshape(state),
        weights.reshape(layers, 9 * channels, channels),
        biases,
        step_sizes,
    )
    return (corrected.reshape(start_states.shape), ends.reshape(start_states.shape))


def solution(mesh):
    in_specs = (
        P("fine", None, "coarse", None, None),
        P("fine", None, None, None),
        P("fine", None),
        P("fine"),
    )
    out_specs = (P("fine", None, "coarse", None, None), P("fine", None, "coarse", None, None))
    return jax.shard_map(local, mesh=mesh, in_specs=in_specs, out_specs=out_specs, check_vma=False)
```

```python
import functools

import jax
import jax.numpy as jnp
from jax import lax
from jax.experimental import pallas as pl
from jax.experimental.pallas import tpu as pltpu
from jax.sharding import PartitionSpec as P

MESH = pl.DeviceIdType.MESH


def kernel(
    slabs,
    bands,
    start,
    stored_weights,
    biases,
    steps,
    corrected,
    ends,
    cols,
    current,
    defect,
    advanced,
    inbox,
    narrow,
    narrow_inbox,
    edge,
    halo,
    row_send,
    row_recv,
    halo_send,
    halo_recv,
    weights,
    load_sem,
):
    rows, width, channels = start.shape
    layers = weights.shape[0]
    own = pl.ds(layers, rows)
    step = 2 if rows % 2 == 0 and layers % 2 == 0 else 1
    state_load = pltpu.make_async_copy(start, current.at[own], load_sem.at[layers])
    state_load.start()

    def weight_load(layer):
        return pltpu.make_async_copy(
            stored_weights.at[layer], weights.at[layer], load_sem.at[layer]
        )

    weight_load(0).start()

    slab = lax.axis_index("fine")
    band = lax.axis_index("coarse")
    total_step = steps[0]
    for layer in range(1, layers):
        total_step = total_step + steps[layer]

    def has_band(side):
        other = band + 2 * side - 1
        return (other >= 0) & (other < bands)

    barrier = pltpu.get_barrier_semaphore()
    around = [(i, j) for i in (-1, 0, 1) for j in (-1, 0, 1) if (i, j) != (0, 0)]
    for i, j in around:
        there = (slab + i >= 0) & (slab + i < slabs) & (band + j >= 0) & (band + j < bands)

        @pl.when(there)
        def _():
            pl.semaphore_signal(
                barrier, inc=1, device_id=(slab + i, band + j), device_id_type=MESH
            )

    def span(at, count):
        return 1 + jnp.where(at > 0, 1, 0) + jnp.where(at < count - 1, 1, 0)

    pl.semaphore_wait(barrier, span(slab, slabs) * span(band, bands) - 1)

    def widened(value):
        count = value.shape[0]
        column = lax.rem(lax.broadcasted_iota(jnp.int32, value.shape, 0), width)
        left = jnp.where(column == 0, 0.0, pltpu.roll(value, 1, 0))
        right = jnp.where(column == width - 1, 0.0, pltpu.roll(value, count - 1, 0))
        return jnp.concatenate([left, value, right], axis=-1).astype(jnp.bfloat16)

    def put(parity, place, value):
        count = value.shape[0] // width
        cols[parity, pl.ds(place, count)] = widened(value).reshape(count, width, 3 * channels)

    def slope(parity, first, count, layer):
        taps = [
            cols[parity, pl.ds(first + a, count)].reshape(count * width, 3 * channels)
            for a in range(3)
        ]
        product = jnp.dot(
            jnp.concatenate(taps, axis=-1), weights[layer], preferred_element_type=jnp.float32
        )
        return jnp.tanh(product + biases[pl.ds(layer, 1), :])

    first_load = pltpu.make_async_copy(start, corrected, load_sem.at[layers + 1])

    @pl.when(slab == 0)
    def _():
        first_load.start()

    def margin_copy(side):
        return pltpu.make_async_remote_copy(
            src_ref=edge.at[side],
            dst_ref=halo.at[0, 1 - side],
            send_sem=halo_send.at[0, side, 0],
            recv_sem=halo_recv.at[0, 1 - side, 0],
            device_id=(slab, band + 2 * side - 1),
            device_id_type=MESH,
        )

    def cross_copy(side, at):
        return pltpu.make_async_remote_copy(
            src_ref=narrow.at[pl.ds(side * (rows - layers) + at, step)],
            dst_ref=halo.at[1, 1 - side, pl.ds(at, step)],
            send_sem=halo_send.at[1, side, at],
            recv_sem=halo_recv.at[1, 1 - side, at],
            device_id=(slab + 1, band + 2 * side - 1),
            device_id_type=MESH,
        )

    def wide_copy(row):
        return pltpu.make_async_remote_copy(
            src_ref=advanced.at[pl.ds(row, step)],
            dst_ref=inbox.at[pl.ds(row, step)],
            send_sem=row_send.at[row],
            recv_sem=row_recv.at[row],
            device_id=(slab + 1, band),
            device_id_type=MESH,
        )

    def narrow_copy(row):
        return pltpu.make_async_remote_copy(
            src_ref=narrow.at[pl.ds(row, step)],
            dst_ref=narrow_inbox.at[pl.ds(row, step)],
            send_sem=row_send.at[row],
            recv_sem=row_recv.at[row],
            device_id=(slab + 1, band),
            device_id_type=MESH,
        )

    odd = lax.rem(slab, 2)

    def send_row(row, value):
        narrow[pl.ds(row, step)] = value.astype(jnp.bfloat16)

        @pl.when(odd == 1)
        def _():
            narrow_copy(row).start()

        @pl.when(odd == 0)
        def _():
            advanced[pl.ds(row, step)] = value
            wide_copy(row).start()

        for side in range(2):
            at = row - side * (rows - layers)

            @pl.when(has_band(side) & (at >= 0) & (at < layers))
            def _():
                cross_copy(side, at).start()

    def set_margin(phase, side, at):
        value = halo[phase, side, at].astype(jnp.float32)
        spot = side * (layers + rows) + at
        current[spot] = value
        put(0, spot, value)

    def take_cross(side, at):
        @pl.when(has_band(side))
        def _():
            pltpu.make_async_remote_copy(
                src_ref=narrow.at[pl.ds(at, step)],
                dst_ref=halo.at[1, side, pl.ds(at, step)],
                send_sem=halo_send.at[1, 1 - side, at],
                recv_sem=halo_recv.at[1, side, at],
                device_id=(slab, band + 2 * side - 1),
                device_id_type=MESH,
            ).wait_recv()
            for more in range(step):
                set_margin(1, side, at + more)

    def layer_step(layer, relaxing):
        margin = layers - 1 - layer
        parity = layer % 2
        if bands == 1:
            first, count = layers, rows
        elif bands == 2:
            first, count = layers - margin * band, rows + margin
        else:
            first, count = layers - margin, rows + 2 * margin
        before = current[pl.ds(first, count)].reshape(count * width, channels)
        slope_term = slope(parity, first - 1, count, layer)
        after = before + steps[layer] * slope_term
        if bands > 2:
            spot = first + lax.broadcasted_iota(jnp.int32, after.shape, 0) // width
            outside = ((band == 0) & (spot < layers)) | (
                (band == bands - 1) & (spot >= layers + rows)
            )
            after = jnp.where(outside, 0.0, after)
        current[pl.ds(first, count)] = after.reshape(count, width, channels)
        if layer < layers - 1:
            put(1 - parity, first, after)
        if relaxing and layer == 0:
            coarse = (before + total_step * slope_term).reshape(count, width, channels)
            if bands == 2:

                @pl.when(band == 0)
                def _():
                    defect[...] = -coarse[:rows]

                @pl.when(band == 1)
                def _():
                    defect[...] = -coarse[margin:]
            else:
                defect[...] = -coarse[layers - first : layers - first + rows]

    for side in range(2):

        @pl.when(~has_band(side))
        def _():
            spots = pl.ds(side * (layers + rows), layers)
            cols[:, spots] = jnp.zeros((2, layers, width, 3 * channels), jnp.bfloat16)
            current[spots] = jnp.zeros((layers, width, channels), jnp.float32)

    state_load.wait()
    for side in range(2):

        @pl.when(has_band(side))
        def _():
            spots = pl.ds(layers + side * (rows - layers), layers)
            edge[side] = current[spots].astype(jnp.bfloat16)
            margin_copy(side).start()

    def load(row, carry):
        put(0, layers + row, current[layers + row])
        return carry

    lax.fori_loop(0, rows, load, 0)
    for side in range(2):

        @pl.when(has_band(side))
        def _():
            pltpu.make_async_remote_copy(
                src_ref=edge.at[1 - side],
                dst_ref=halo.at[0, side],
                send_sem=halo_send.at[0, 1 - side, 0],
                recv_sem=halo_recv.at[0, side, 0],
                device_id=(slab, band + 2 * side - 1),
                device_id_type=MESH,
            ).wait_recv()
            for at in range(layers):
                set_margin(0, side, at)

    for layer in range(layers):
        weight_load(layer).wait()
        if layer < layers - 1:
            weight_load(layer + 1).start()
        layer_step(layer, True)
    defect[...] += current[own]

    near = 1 - lax.rem(band, 2)
    far = 1 - near

    def place(at):
        return near * (rows - step) + (1 - 2 * near) * at * step

    def next_to(side):
        return (1 - side) * (layers - step)

    @pl.when(slab == 0)
    def _():
        if slabs > 1:

            def hand_on(at, carry):
                row = place(at)
                send_row(row, current[pl.ds(layers + row, step)])
                return carry

            lax.fori_loop(0, rows // step, hand_on, 0)
        first_load.wait()
        ends[...] = current[own]

    @pl.when(slab > 0)
    def _():
        def take_row(row):
            @pl.when(odd == 1)
            def _():
                wide_copy(row).wait_recv()

            @pl.when(odd == 0)
            def _():
                narrow_copy(row).wait_recv()
                inbox[pl.ds(row, step)] = narrow_inbox[pl.ds(row, step)].astype(jnp.float32)

            put(0, layers + row, inbox[pl.ds(row, step)].reshape(step * width, channels))

        group = (step, width, channels)
        take_row(place(0))
        take_cross(near, next_to(near))

        def chain(at, carry):
            row = place(at)

            @pl.when(at < rows // step - 1)
            def _():
                take_row(place(at + 1))

            @pl.when(at == rows // step - 1)
            def _():
                take_cross(far, next_to(far))

            slope_term = slope(0, layers + row - 1, step, 0).reshape(group)
            value = inbox[pl.ds(row, step)]

            @pl.when(slab < slabs - 1)
            def _():
                send_row(row, value + total_step * slope_term + defect[pl.ds(row, step)])

            after = value + steps[0] * slope_term
            current[pl.ds(layers + row, step)] = after
            put(1, layers + row, after.reshape(step * width, channels))
            corrected[pl.ds(row, step)] = value
            return carry

        lax.fori_loop(0, rows // step, chain, 0)
        if layers > 1:
            for side in range(2):
                for at in range(0, layers, step):
                    if at != next_to(side):
                        take_cross(side, at)

                @pl.when(has_band(side))
                def _():
                    first = 1 + side * (layers + rows - 1)
                    count = layers - 1
                    before = current[pl.ds(first, count)].reshape(count * width, channels)
                    after = before + steps[0] * slope(0, first - 1, count, 0)
                    current[pl.ds(first, count)] = after.reshape(count, width, channels)
                    put(1, first, after)

            for layer in range(1, layers):
                layer_step(layer, False)
        ends[...] = current[own]

    for side in range(2):

        @pl.when(has_band(side))
        def _():
            margin_copy(side).wait_send()

            @pl.when(slab < slabs - 1)
            def _():
                for at in range(0, layers, step):
                    cross_copy(side, at).wait_send()

    @pl.when((slab < slabs - 1) & (odd == 1))
    def _():
        for row in range(0, rows, step):
            narrow_copy(row).wait_send()

    @pl.when((slab < slabs - 1) & (odd == 0))
    def _():
        for row in range(0, rows, step):
            wide_copy(row).wait_send()


def local(start_states, weights, biases, step_sizes):
    rows, width, channels = start_states.shape[2:]
    layers = weights.shape[0]
    state = (rows, width, channels)
    anywhere = pl.BlockSpec(memory_space=pl.ANY)
    whole = pl.BlockSpec(memory_space=pltpu.VMEM)
    shape = jax.ShapeDtypeStruct(state, jnp.float32)
    corrected, ends = pl.pallas_call(
        functools.partial(kernel, lax.axis_size("fine"), lax.axis_size("coarse")),
        out_shape=(shape, shape),
        in_specs=[anywhere, anywhere, whole, pl.BlockSpec(memory_space=pltpu.SMEM)],
        out_specs=(whole, whole),
        scratch_shapes=[
            pltpu.VMEM((2, rows + 2 * layers, width, 3 * channels), jnp.bfloat16),
            pltpu.VMEM((rows + 2 * layers, width, channels), jnp.float32),
            pltpu.VMEM(state, jnp.float32),
            pltpu.VMEM(state, jnp.float32),
            pltpu.VMEM(state, jnp.float32),
            pltpu.VMEM(state, jnp.bfloat16),
            pltpu.VMEM(state, jnp.bfloat16),
            pltpu.VMEM((2, layers, width, channels), jnp.bfloat16),
            pltpu.VMEM((2, 2, layers, width, channels), jnp.bfloat16),
            pltpu.SemaphoreType.DMA((rows,)),
            pltpu.SemaphoreType.DMA((rows,)),
            pltpu.SemaphoreType.DMA((2, 2, layers)),
            pltpu.SemaphoreType.DMA((2, 2, layers)),
            pltpu.VMEM((layers, 9 * channels, channels), jnp.bfloat16),
            pltpu.SemaphoreType.DMA((layers + 2,)),
        ],
        compiler_params=pltpu.CompilerParams(
            collective_id=0, has_side_effects=True, vmem_limit_bytes=52 * 1024 * 1024
        ),
    )(
        start_states.reshape(state),
        weights.reshape(layers, 9 * channels, channels),
        biases,
        step_sizes,
    )
    return (corrected.reshape(start_states.shape), ends.reshape(start_states.shape))


def solution(mesh):
    in_specs = (
        P("fine", None, "coarse", None, None),
        P("fine", None, None, None),
        P("fine", None),
        P("fine"),
    )
    out_specs = (P("fine", None, "coarse", None, None), P("fine", None, "coarse", None, None))
    return jax.shard_map(local, mesh=mesh, in_specs=in_specs, out_specs=out_specs, check_vma=False)
```
